1024 devices in a mesh: ctx: 8 (over y), exp: 16 (over z), etp: 8 (over x, core).
Axes of the slice: x: 4, y: 8, z: 16, core: 2. Of those that a mesh axis runs over, the one named last changes fastest.
Arguments:
- tokens: bfloat16 [4096, 4096], P(('ctx', 'exp'), 'etp'), may hold values from -6 to 6
- grad_out: bfloat16 [4096, 4096], P(('ctx', 'exp'), 'etp'), may hold values from -6 to 6
- route_weight: float32 [4096, 1], P(('ctx', 'exp')), may hold values from 0.1 to 1
- routes: int32 [4096, 1], P(('ctx', 'exp')), may hold values from 0 to 3; in each aligned block of 32 rows (0 to 31, 32 to 63, ...) at most 16 rows name the same one
- w_gate: bfloat16 [21504, 4096], P(('exp', 'etp')), may hold values from -0.09375 to 0.09375
- w_up: bfloat16 [21504, 4096], P(('exp', 'etp')), may hold values from -0.09375 to 0.09375
- w_down: bfloat16 [21504, 4096], P(('exp', 'etp')), may hold values from -0.078125 to 0.078125
Outputs:
- d_tokens: bfloat16 [4096, 4096], P(('ctx', 'exp'), 'etp')
- d_w_gate: bfloat16 [21504, 4096], P(('exp', 'etp'), 'ctx')
- d_w_up: bfloat16 [21504, 4096], P(('exp', 'etp'), 'ctx')
- d_w_down: bfloat16 [21504, 4096], P(('exp', 'etp'), 'ctx')
The draws below stay inside these ranges and needn't reach their ends.
Inputs may be any that keep to these rules, and one draw needn't show every extreme that they name: `routes`: within each aligned block of 32 tokens (the tokens of one index pair of ctx and exp) at most 16 name the same expert; in every draw some block has exactly 16 naming one expert.
All inputs are finite; a program needn't handle non-finite values.
Results may differ from the reference program's by a relative error of at most 0.02.
Values may be sent and summed in bfloat16 or wider, within the bound.
A program may use at most 64 MiB of HBM per device.

```python
import math
import jax
import jax.numpy as jnp
import numpy as np
from jax import lax

D = 4096
FF = 5376
EXPERTS = 4
TOK_DEV = 32
MOST = 16
TOKENS = 4096
N_CTX = 8
N_EXP = 16


def block_levels(rng, dims, split, least, top_value):
    level = 1.0
    for position, parts in split:
        steps = jax.random.uniform(jax.random.fold_in(jax.random.fold_in(rng, 6), position), (parts,), jnp.float32, least / len(split), top_value / len(split))
        level = level * jnp.repeat(jnp.exp(steps), dims[position] // parts).reshape((-1,) + (1,) * (len(dims) - 1 - position))
    return level


def shared_out(rng, own, number, rows, number_of, top, most, skew):
    sequence = jax.random.permutation(rng, number_of)
    packed, ordinary = portions_of(number_of, rows * top, most, skew, True), portions_of(number_of, rows * top, most, skew, False)
    places = jnp.arange(number_of)

    def named(sizes, offset_by):
        used = int((sizes > 0).sum())
        fixed = max(1, used // 4)
        passed = fixed + (places - fixed + offset_by * (used - fixed)) % max(1, number_of - fixed)
        return jnp.zeros((number_of,), jnp.int32).at[sequence[jnp.where(places < fixed, places, passed)]].set(jnp.asarray(sizes, jnp.int32))

    sizes = jnp.where(number % 4 == 0, named(packed, number // 4), named(ordinary, number - number // 4 - 1))
    mixed = jax.random.permutation(jax.random.fold_in(own, 3), number_of)
    giver, taker = mixed[0:number_of // 2 * 2:2], mixed[1:number_of // 2 * 2:2]
    slack = jnp.minimum(sizes[giver] - 1, most - sizes[taker]) // 2
    slack = jnp.where((giver == sequence[0]) | (taker == sequence[0]) | (sizes[taker] == 0), 0, jnp.maximum(slack, 0))
    passed = jax.random.randint(jax.random.fold_in(own, 4), (number_of // 2,), 0, 1 << 20) % (slack + 1)
    sizes = sizes.at[giver].add(-passed).at[taker].add(passed)
    members = jnp.searchsorted(jnp.cumsum(sizes), jnp.arange(rows * top), side="right").astype(jnp.int32)
    grid = members.reshape(top, rows).T
    grid = grid[jax.random.permutation(jax.random.fold_in(own, 1), rows)]
    offset_by = jax.random.randint(jax.random.fold_in(own, 2), (rows, 1), 0, top)
    return jnp.take_along_axis(grid, (jnp.arange(top)[None, :] + offset_by) % top, axis=1)


def portions_of(number_of, total, limit, slope, full):
    loads = [(1 << 20) // math.isqrt(rank ** slope) + 1 for rank in range(1, number_of + 1)]
    largest = limit if full else min(limit, max(-(-total // number_of), total * loads[0] // sum(loads)))
    least = 1 if total - largest >= number_of - 1 else 0
    given, surplus = [largest] + [least] * (number_of - 1), total - largest - least * (number_of - 1)
    while surplus > 0:
        movable = [i for i in range(1, number_of) if given[i] < largest] or [i for i in range(1, number_of) if given[i] < limit]
        mass, budget = sum([loads[i] for i in movable]), surplus
        for i in movable:
            more = min(limit - given[i], max(1, budget * loads[i] // mass), surplus)
            given[i] = given[i] + more
            surplus = surplus - more
    return np.array(given)


def centred(stream_key, dims, scale, bound, cuts=(), held_as=jnp.bfloat16):
    gain = block_levels(stream_key, dims, cuts, -0.22, 0.18) if cuts else 1.0
    entries = jax.random.normal(stream_key, dims, jnp.float32) * scale * gain
    return jnp.minimum(jnp.maximum(entries, -bound), bound).astype(held_as)


def setup_inputs(seed: int = 0) -> dict:
    splits = jax.random.split(jax.random.key(seed), 8)
    tokens = centred(splits[0], (TOKENS, D), 1.0, 6.0, ((0, 128), (1, 8)))
    grad_out = centred(splits[1], (TOKENS, D), 1.0, 6.0, ((0, 128), (1, 8)))
    route_weight = jnp.clip(jnp.exp(math.log(1.0) - 2.3025851 * jax.random.uniform(splits[2], (TOKENS, 1), jnp.float32) ** block_levels(splits[2], (TOKENS, 1), ((0, 128),), -0.2, 0.2)), 0.1, 1.0)
    routes_keys = jax.random.split(jax.random.fold_in(splits[3], 1), TOKENS // TOK_DEV)
    routes_turns = jax.random.permutation(jax.random.fold_in(splits[3], 3), TOKENS // TOK_DEV)
    routes = jax.vmap(lambda own, number: shared_out(jax.random.fold_in(splits[3], 2), own, number, TOK_DEV, EXPERTS, 1, MOST, 2))(routes_keys, routes_turns).reshape((TOKENS, 1))
    w_gate = centred(splits[4], (EXPERTS * FF, D), D ** -0.5, 0.09375, ((0, 128),))
    w_up = centred(splits[5], (EXPERTS * FF, D), D ** -0.5, 0.09375, ((0, 128),))
    w_down = centred(splits[6], (EXPERTS * FF, D), FF ** -0.5, 0.078125, ((0, 128),))
    return dict(tokens=tokens, grad_out=grad_out, route_weight=route_weight, routes=routes, w_gate=w_gate, w_up=w_up, w_down=w_down)


def reference(tokens, grad_out, route_weight, routes, w_gate, w_up, w_down):
    group_rows = TOKENS // N_CTX
    slot_total = N_EXP * MOST
    scaled = (route_weight * grad_out.astype(jnp.float32)).astype(jnp.bfloat16)
    gate_sums = [jnp.zeros((FF, D), jnp.float32) for expert_index in range(EXPERTS)]
    up_sums = [jnp.zeros((FF, D), jnp.float32) for expert_index in range(EXPERTS)]
    down_sums = [jnp.zeros((FF, D), jnp.float32) for expert_index in range(EXPERTS)]
    token_grads = []
    for group_index in range(N_CTX):
        row_lower = group_index * group_rows
        padded_tokens = jnp.concatenate([tokens[row_lower:row_lower + group_rows], jnp.zeros((1, D), tokens.dtype)], axis=0)
        padded_scaled = jnp.concatenate([scaled[row_lower:row_lower + group_rows], jnp.zeros((1, D), scaled.dtype)], axis=0)
        route_group = routes[row_lower:row_lower + group_rows, 0]
        group_grad = jnp.zeros((group_rows + 1, D), jnp.float32)
        for expert_index in range(EXPERTS):
            picked = jnp.nonzero(route_group == expert_index, size=slot_total, fill_value=group_rows)[0].astype(jnp.int32)
            rows_in = padded_tokens[picked]
            grads_in = padded_scaled[picked]
            row_start = expert_index * FF
            gate_rows = w_gate[row_start:row_start + FF]
            up_rows = w_up[row_start:row_start + FF]
            down_rows = w_down[row_start:row_start + FF]
            gate_pre = jnp.dot(rows_in, gate_rows.T, preferred_element_type=jnp.float32)
            up_pre = jnp.dot(rows_in, up_rows.T, preferred_element_type=jnp.float32)
            gate_sigmoid = jax.nn.sigmoid(gate_pre)
            activated = gate_pre * gate_sigmoid
            hidden = (activated * up_pre).astype(jnp.bfloat16)
            d_hidden = jnp.dot(grads_in, down_rows.T, preferred_element_type=jnp.float32)
            d_gate_act = (d_hidden * up_pre * gate_sigmoid * (1.0 + gate_pre * (1.0 - gate_sigmoid))).astype(jnp.bfloat16)
            d_up_act = (d_hidden * activated).astype(jnp.bfloat16)
            d_rows = jnp.dot(d_gate_act, gate_rows, preferred_element_type=jnp.float32) + jnp.dot(d_up_act, up_rows, preferred_element_type=jnp.float32)
            group_grad = group_grad.at[picked].add(d_rows)
            part_gate = lax.optimization_barrier(jnp.dot(d_gate_act.T, rows_in, preferred_element_type=jnp.float32).astype(jnp.bfloat16))
            part_up = lax.optimization_barrier(jnp.dot(d_up_act.T, rows_in, preferred_element_type=jnp.float32).astype(jnp.bfloat16))
            part_down = lax.optimization_barrier(jnp.dot(hidden.T, grads_in, preferred_element_type=jnp.float32).astype(jnp.bfloat16))
            gate_sums[expert_index] = gate_sums[expert_index] + part_gate.astype(jnp.float32)
            up_sums[expert_index] = up_sums[expert_index] + part_up.astype(jnp.float32)
            down_sums[expert_index] = down_sums[expert_index] + part_down.astype(jnp.float32)
        token_grads.append(group_grad[:group_rows])
    d_tokens = jnp.concatenate(token_grads, axis=0).astype(jnp.bfloat16)
    d_w_gate = jnp.concatenate(gate_sums, axis=0).astype(jnp.bfloat16)
    d_w_up = jnp.concatenate(up_sums, axis=0).astype(jnp.bfloat16)
    d_w_down = jnp.concatenate(down_sums, axis=0).astype(jnp.bfloat16)
    return (d_tokens, d_w_gate, d_w_up, d_w_down)
```

```python
import jax
import jax.numpy as jnp
from jax import lax
from jax.sharding import PartitionSpec as P

EXPERTS = 4
MOST = 16


def on_device(tokens, grad_out, route_weight, routes, w_gate, w_up, w_down):
    n_exp = lax.axis_size("exp")
    group_split = n_exp // EXPERTS
    rows = tokens.shape[0]
    feats = tokens.shape[1]
    hid_dev = w_gate.shape[0]
    my_expert = lax.axis_index("exp") // group_split
    scaled = (route_weight * grad_out.astype(jnp.float32)).astype(jnp.bfloat16)
    tagged = jnp.broadcast_to(routes.astype(jnp.bfloat16), (rows, 128))
    packed = lax.all_gather(
        jnp.concatenate([tokens, scaled, tagged], axis=1), "exp", axis=0, tiled=True
    )
    expert_all = packed[:, 2 * feats].astype(jnp.int32).reshape(n_exp, rows)
    mine = (expert_all == my_expert).astype(jnp.int32)
    rank = jnp.cumsum(mine, axis=1) - 1
    slot = jnp.where(mine == 1, rank, -1)
    pick = (slot[:, None, :] == jnp.arange(MOST, dtype=jnp.int32)[None, :, None]).astype(jnp.bfloat16)
    chosen = lax.dot_general(
        pick,
        packed[:, : 2 * feats].reshape(n_exp, rows, 2 * feats),
        (((2,), (1,)), ((0,), (0,))),
        preferred_element_type=jnp.float32,
    ).astype(jnp.bfloat16)
    slots = n_exp * MOST
    chosen = chosen.reshape(slots, 2, feats)
    full = lax.all_gather(chosen, "etp", axis=0, tiled=False)
    full_t = full.transpose(2, 1, 0, 3).reshape(2, slots, -1)
    rows_in, grads_in = full_t[0], full_t[1]
    full_width = rows_in.shape[1]
    across = (((1,), (1,)), ((), ()))
    gate_pre = lax.dot_general(rows_in, w_gate, across, preferred_element_type=jnp.float32)
    up_pre = lax.dot_general(rows_in, w_up, across, preferred_element_type=jnp.float32)
    gate_sigmoid = jax.nn.sigmoid(gate_pre)
    activated = gate_pre * gate_sigmoid
    hidden = (activated * up_pre).astype(jnp.bfloat16)
    d_hidden = lax.dot_general(grads_in, w_down, across, preferred_element_type=jnp.float32)
    d_gate_act = (
        d_hidden * up_pre * gate_sigmoid * (1.0 + gate_pre * (1.0 - gate_sigmoid))
    ).astype(jnp.bfloat16)
    d_up_act = (d_hidden * activated).astype(jnp.bfloat16)
    d_slots = jnp.dot(d_gate_act, w_gate, preferred_element_type=jnp.float32) + jnp.dot(
        d_up_act, w_up, preferred_element_type=jnp.float32
    )
    part = lax.psum_scatter(d_slots.astype(jnp.bfloat16), "etp", scatter_dimension=1, tiled=True)
    returned = lax.all_to_all(
        part.reshape(n_exp, MOST, feats), "exp", split_axis=0, concat_axis=0, tiled=True
    ).astype(jnp.float32)
    merged = (
        returned.reshape(EXPERTS, group_split, MOST, feats)
        .sum(axis=1)
        .reshape(EXPERTS * MOST, feats)
        .astype(jnp.bfloat16)
    )
    expert_ids = routes[:, 0]
    member = (expert_ids[:, None] == jnp.arange(EXPERTS, dtype=jnp.int32)[None, :]).astype(jnp.int32)
    ranking = jnp.sum((jnp.cumsum(member, axis=0) - 1) * member, axis=1)
    position = expert_ids * MOST + ranking
    place = (position[:, None] == jnp.arange(EXPERTS * MOST, dtype=jnp.int32)[None, :]).astype(jnp.bfloat16)
    d_tokens = jnp.dot(place, merged, preferred_element_type=jnp.float32).astype(jnp.bfloat16)
    leading = (((0,), (0,)), ((), ()))
    weight_sums = lax.psum_scatter(
        jnp.concatenate(
            [
                lax.dot_general(rows_in, d_gate_act, leading, preferred_element_type=jnp.float32),
                lax.dot_general(rows_in, d_up_act, leading, preferred_element_type=jnp.float32),
                lax.dot_general(grads_in, hidden, leading, preferred_element_type=jnp.float32),
            ],
            axis=1,
        ).astype(jnp.bfloat16),
        "ctx",
        scatter_dimension=0,
        tiled=True,
    ).astype(jnp.float32)
    d_w_gate = weight_sums[:, :hid_dev].T.astype(jnp.bfloat16)
    d_w_up = weight_sums[:, hid_dev : 2 * hid_dev].T.astype(jnp.bfloat16)
    d_w_down = weight_sums[:, 2 * hid_dev :].T.astype(jnp.bfloat16)
    return (d_tokens, d_w_gate, d_w_up, d_w_down)


def solution(mesh):
    in_specs = (
        P(("ctx", "exp"), "etp"),
        P(("ctx", "exp"), "etp"),
        P(("ctx", "exp"), None),
        P(("ctx", "exp"), None),
        P(("exp", "etp"), None),
        P(("exp", "etp"), None),
        P(("exp", "etp"), None),
    )
    out_specs = (
        P(("ctx", "exp"), "etp"),
        P(("exp", "etp"), "ctx"),
        P(("exp", "etp"), "ctx"),
        P(("exp", "etp"), "ctx"),
    )
    return jax.shard_map(
        on_device, mesh=mesh, in_specs=in_specs, out_specs=out_specs, check_vma=False
    )
```

```python
import functools

import jax
import jax.numpy as jnp
from jax import lax
from jax.experimental import pallas as pl
from jax.experimental.pallas import tpu as pltpu
from jax.sharding import PartitionSpec as P

EXPERTS = 4
MOST = 16
TAG = 128
LANES = 4
LAG_NEAR = 2
LAG_FAR = 4
MESH = pl.DeviceIdType.MESH
F32 = jnp.float32
BF16 = jnp.bfloat16
ACROSS = (((1,), (1,)), ((), ()))
LEADING = (((0,), (0,)), ((), ()))


def aligned(index, size):
    return pl.ds(pl.multiple_of(index * size, size), size)


def kernel(
    n_ctx,
    n_exp,
    n_etp,
    tok_ref,
    grad_ref,
    weight_ref,
    routes_ref,
    gate_hbm,
    up_hbm,
    down_hbm,
    d_tok_ref,
    d_gate_ref,
    d_up_ref,
    d_down_ref,
    raw,
    x,
    w_gate,
    w_up,
    w_down,
    acts,
    total,
    y_out,
    y_in,
    pair_out,
    pair_in,
    far_out,
    far_in,
    near_sum,
    near_out,
    near_in,
    home_out,
    home_in,
    w_sem,
    z_send,
    z_recv,
    x_send,
    x_recv,
    y_send,
    y_recv,
    pair_send,
    pair_recv,
    far_send,
    far_recv,
    near_send,
    near_recv,
    home_send,
    home_recv,
):
    rows, feats = tok_ref.shape
    hid = w_gate.shape[0]
    half = rows // 2
    n_x = n_etp // 2
    group_split = n_exp // EXPERTS
    chunks = n_exp // 2
    slots = n_exp * MOST
    c = lax.axis_index("ctx")
    z = lax.axis_index("exp")
    t = lax.axis_index("etp")
    xx = t // 2
    core = t % 2
    sib = t + 1 - 2 * core
    expert = z // group_split

    def along_x(step):
        return ((xx + step) % n_x) * 2 + core

    right, left, far = along_x(1), along_x(n_x - 1), along_x(2)
    z_next, z_prev = (z + 1) % n_exp, (z + n_exp - 1) % n_exp
    y_next, y_prev = (c + 1) % n_ctx, (c + n_ctx - 1) % n_ctx

    loads = [
        pltpu.make_async_copy(src, dst, w_sem.at[i])
        for i, (src, dst) in enumerate(((gate_hbm, w_gate), (up_hbm, w_up), (down_hbm, w_down)))
    ]
    for load in loads:
        load.start()

    barrier = pltpu.get_barrier_semaphore()
    partners = [{"etp": right}, {"etp": left}, {"etp": sib}, {"ctx": y_next}, {"ctx": y_prev}]
    partners += [{"exp": (z + k) % n_exp} for k in range(1, n_exp)]
    for partner in partners:
        pl.semaphore_signal(barrier, inc=1, device_id=partner, device_id_type=MESH)

    expert_col = routes_ref[...]
    lane = lax.broadcasted_iota(jnp.int32, (rows, TAG), 1)
    one_hot = (lane == expert_col).astype(BF16)
    earlier = (
        lax.broadcasted_iota(jnp.int32, (rows, rows), 0)
        > lax.broadcasted_iota(jnp.int32, (rows, rows), 1)
    ).astype(BF16)
    before = jnp.dot(earlier, one_hot, preferred_element_type=F32)
    rank = jnp.sum(before * one_hot.astype(F32), axis=1, keepdims=True)
    position = expert_col.astype(F32) * MOST + rank
    raw[:rows, :feats] = tok_ref[...]
    raw[:rows, feats : 2 * feats] = (weight_ref[...] * grad_ref[...].astype(F32)).astype(BF16)
    raw[:rows, 2 * feats :] = jnp.broadcast_to(position, (rows, TAG)).astype(BF16)

    pl.semaphore_wait(barrier, len(partners))

    def send(src, dst, send_sem, recv_sem, target):
        return pltpu.make_async_remote_copy(
            src_ref=src,
            dst_ref=dst,
            send_sem=send_sem,
            recv_sem=recv_sem,
            device_id=target,
            device_id_type=MESH,
        )

    def raw_half(block, part):
        return raw.at[aligned(2 * block + part, half)]

    def z_copy(src, dst, part, target):
        return send(
            raw_half(src, part),
            raw_half(dst, part),
            z_send.at[dst, part],
            z_recv.at[dst, part],
            {"exp": target},
        )

    for part in range(2):
        z_copy(0, 1, part, z_next).start()
        z_copy(0, 2, part, z_prev).start()

    def piece(k, owner):
        return x.at[:, aligned(k, 2 * MOST), aligned(owner, feats)]

    def piece_of(kind, k, owner):
        return x.at[kind, aligned(k, 2 * MOST), aligned(owner, feats)]

    def x_copy(which, k):
        if which == 0:
            ref, target = piece(k, t), right
        elif which == 1:
            ref, target = piece(k, t), left
        elif which == 2:
            ref, target = piece(k, t), sib
        elif which == 3:
            ref, target = piece_of(0, k, left), right
        elif which == 4:
            ref, target = piece_of(1, k, right), left
        elif which == 5:
            ref, target = piece(k, left), sib
        elif which == 6:
            ref, target = piece(k, right), sib
        elif which == 7:
            ref, target = piece_of(0, k, far), sib
        else:
            ref, target = piece_of(1, k, far), sib
        return send(ref, ref, x_send.at[which, k], x_recv.at[which, k], {"etp": target})

    def x_arrive(which, k):
        turn = 1 - 2 * core
        if which == 0:
            ref = piece(k, left)
        elif which == 1:
            ref = piece(k, right)
        elif which == 2:
            ref = piece(k, sib)
        elif which == 3:
            ref = piece_of(0, k, far)
        elif which == 4:
            ref = piece_of(1, k, far)
        elif which == 5:
            ref = piece(k, left + turn)
        elif which == 6:
            ref = piece(k, right + turn)
        elif which == 7:
            ref = piece_of(0, k, far + turn)
        else:
            ref = piece_of(1, k, far + turn)
        send(ref, ref, x_send.at[which, k], x_recv.at[which, k], {"etp": sib}).wait_recv()

    pick_row = lax.broadcasted_iota(jnp.int32, (2 * rows, 2 * MOST), 0)
    pick_lane = lax.broadcasted_iota(jnp.int32, (2 * rows, 2 * MOST), 1)

    def dispatch(i, carry):
        @pl.when(i < chunks)
        def _():
            forth, back = 2 * i + 1, 2 * i + 2
            for part in range(2):
                z_copy(forth, forth, part, z_next).wait_recv()

                @pl.when(i < chunks - 1)
                def _():
                    z_copy(forth, forth + 2, part, z_next).start()
                    z_copy(back, back, part, z_prev).wait_recv()

                @pl.when(i < chunks - 2)
                def _():
                    z_copy(back, back + 2, part, z_prev).start()

            block = raw[aligned(i, 2 * rows), :]
            tag = block[:, 2 * feats : 2 * feats + 2 * MOST].astype(jnp.int32) - expert * MOST
            spot = jnp.where(pick_row >= rows, tag + MOST, tag)
            pick = jnp.where((tag >= 0) & (tag < MOST) & (spot == pick_lane), 1.0, 0.0).astype(BF16)
            chosen = lax.dot_general(
                pick, block[:, : 2 * feats], LEADING, preferred_element_type=F32
            ).astype(BF16)
            x[0, aligned(i, 2 * MOST), aligned(t, feats)] = chosen[:, :feats]
            x[1, aligned(i, 2 * MOST), aligned(t, feats)] = chosen[:, feats:]
            for which in range(3):
                x_copy(which, i).start()

        @pl.when((i >= LAG_NEAR) & (i < chunks + LAG_NEAR))
        def _():
            k = i - LAG_NEAR
            x_arrive(0, k)
            x_copy(3, k).start()
            x_copy(5, k).start()
            x_arrive(1, k)
            x_copy(4, k).start()
            x_copy(6, k).start()

        @pl.when(i >= LAG_FAR)
        def _():
            k = i - LAG_FAR
            x_arrive(3, k)
            x_copy(7, k).start()
            x_arrive(4, k)
            x_copy(8, k).start()

        return carry

    lax.fori_loop(0, chunks + LAG_FAR, dispatch, 0)

    def gathered(k, carry):
        for which in (2, 5, 6, 7, 8):
            x_arrive(which, k)
        for which in range(9):
            x_copy(which, k).wait_send()
        return carry

    lax.fori_loop(0, chunks, gathered, 0)
    for load in loads:
        load.wait()

    tok_all, grad_all = x[0], x[1]
    gate = lax.dot_general(w_gate[...], tok_all, ACROSS, preferred_element_type=F32)
    up = lax.dot_general(w_up[...], tok_all, ACROSS, preferred_element_type=F32)
    d_hidden = lax.dot_general(w_down[...], grad_all, ACROSS, preferred_element_type=F32)
    sig = jax.nn.sigmoid(gate)
    activated = gate * sig
    hidden = activated * up
    d_gate = d_hidden * up * sig * (1.0 + gate * (1.0 - sig))
    d_up = d_hidden * activated
    acts_rows = acts.shape[0]
    acts[...] = jnp.concatenate(
        [d_gate, d_up, hidden, jnp.zeros((acts_rows - 3 * hid, slots), F32)], axis=0
    ).astype(BF16)
    wide = -(-hid // 128) * 128
    fill = jnp.zeros((wide - hid, slots), F32)
    gate_act = jnp.concatenate([d_gate, fill], axis=0).T.astype(BF16)[:, :hid]
    up_act = jnp.concatenate([d_up, fill], axis=0).T.astype(BF16)[:, :hid]

    lane_rows = acts_rows // LANES

    def weight_part(number, owner):
        low, high = number * lane_rows, (number + 1) * lane_rows
        cols = aligned(owner, feats)
        parts = []
        if low < 2 * hid:
            parts.append(
                jnp.dot(acts[low : min(high, 2 * hid), :], x[0, :, cols], preferred_element_type=F32)
            )
        if high > 2 * hid:
            parts.append(
                jnp.dot(acts[max(low, 2 * hid) : high, :], x[1, :, cols], preferred_element_type=F32)
            )
        return parts[0] if len(parts) == 1 else jnp.concatenate(parts, axis=0)

    def y_copy(number, step):
        target = y_next if number < LANES // 2 else y_prev
        return send(
            y_out.at[number, step],
            y_in.at[number, step],
            y_send.at[number, step],
            y_recv.at[number, step],
            {"ctx": target},
        )

    def y_step(step):
        for number in (0, 2, 1, 3):
            if number < LANES // 2:
                owner = (c + 2 * n_ctx - 1 - step) % n_ctx
            else:
                owner = (c + 1 + step) % n_ctx
            value = weight_part(number, owner)
            if step > 0:
                y_copy(number, step - 1).wait_recv()
                value = value + y_in[number, step - 1].astype(F32)
            y_out[number, step] = value.astype(BF16)
            y_copy(number, step).start()

    def y_last():
        for number in (0, 2, 1, 3):
            value = weight_part(number, c)
            y_copy(number, n_ctx - 2).wait_recv()
            total[number * lane_rows : (number + 1) * lane_rows, :] = value + y_in[
                number, n_ctx - 2
            ].astype(F32)
        d_gate_ref[...] = total[:hid, :].astype(BF16)
        d_up_ref[...] = total[hid : 2 * hid, :].astype(BF16)
        d_down_ref[...] = total[2 * hid : 3 * hid, :].astype(BF16)

    def slot_part(owner):
        cols = aligned(owner, feats)
        return jnp.dot(gate_act, w_gate[:, cols], preferred_element_type=F32) + jnp.dot(
            up_act, w_up[:, cols], preferred_element_type=F32
        )

    def pair_copy(i):
        return send(
            pair_out.at[i], pair_in.at[i], pair_send.at[i], pair_recv.at[i], {"etp": sib}
        )

    middle = slots // 2

    def far_copy(side):
        return send(
            far_out.at[pl.ds(side * middle, middle)],
            far_in.at[side],
            far_send.at[side],
            far_recv.at[side],
            {"etp": left if side else right},
        )

    def near_copy(side):
        return send(
            near_out.at[side],
            near_in.at[side],
            near_send.at[side],
            near_recv.at[side],
            {"etp": left if side else right},
        )

    def to_pair():
        for i in (2, 1, 3, 0):
            pair_out[i] = slot_part(((xx + i) % n_x) * 2 + 1 - core).astype(BF16)
            pair_copy(i).start()

    def pair_sum(i):
        value = slot_part(along_x(i))
        pair_copy(i).wait_recv()
        return value + pair_in[i].astype(F32)

    def to_far():
        far_out[...] = pair_sum(2).astype(BF16)
        far_copy(0).start()
        far_copy(1).start()
        near_sum[0] = pair_sum(1)
        near_sum[1] = pair_sum(n_x - 1)

    def to_near():
        far_copy(0).wait_recv()
        near_out[0, :middle, :] = (near_sum[0, :middle, :] + far_in[0].astype(F32)).astype(BF16)
        near_out[0, middle:, :] = near_sum[0, middle:, :].astype(BF16)
        near_copy(0).start()
        far_copy(1).wait_recv()
        near_out[1, :middle, :] = near_sum[1, :middle, :].astype(BF16)
        near_out[1, middle:, :] = (near_sum[1, middle:, :] + far_in[1].astype(F32)).astype(BF16)
        near_copy(1).start()
        near_sum[2] = pair_sum(0)

    def shift(block):
        k = (block + 1) // 2
        return -k if block % 2 else k

    def home_copy(block):
        return send(
            home_out.at[pl.ds(block * MOST, MOST)],
            home_in.at[z],
            home_send.at[block],
            home_recv.at[block],
            {"exp": (z + shift(block) + n_exp) % n_exp},
        )

    def to_home():
        near_copy(0).wait_recv()
        near_copy(1).wait_recv()
        home_out[...] = (
            near_sum[2] + near_in[0].astype(F32) + near_in[1].astype(F32)
        ).astype(BF16)
        for block in range(1, n_exp):
            home_copy(block).start()
        home_in[z] = home_out[:MOST, :]

    def at_home():
        for block in range(1, n_exp):
            source = (z - shift(block) + n_exp) % n_exp
            ref = home_in.at[source]
            send(ref, ref, home_send.at[block], home_recv.at[block], {"exp": source}).wait_recv()
        merged = []
        for e in range(EXPERTS):
            value = home_in[e * group_split].astype(F32)
            for j in range(1, group_split):
                value = value + home_in[e * group_split + j].astype(F32)
            merged.append(value)
        merged = jnp.concatenate(merged, axis=0).astype(BF16)
        spots = EXPERTS * MOST
        place = jnp.where(
            lax.broadcasted_iota(jnp.int32, (rows, spots), 1) == position.astype(jnp.int32), 1.0, 0.0
        ).astype(BF16)
        d_tok_ref[...] = jnp.dot(place, merged, preferred_element_type=F32).astype(BF16)

    between = {0: to_pair, 1: to_far, 2: to_near, 3: to_home, 5: at_home}
    for step in range(n_ctx - 1):
        y_step(step)
        if step in between:
            between[step]()
    for step in sorted(between):
        if step >= n_ctx - 1:
            between[step]()
    y_last()

    for block in range(1, n_exp):
        for part in range(2):
            z_copy(block, block, part, z_next).wait_send()
        home_copy(block).wait_send()
    for number in range(LANES):
        for step in range(n_ctx - 1):
            y_copy(number, step).wait_send()
    for i in range(n_x):
        pair_copy(i).wait_send()
    for side in range(2):
        far_copy(side).wait_send()
        near_copy(side).wait_send()


def on_device(tokens, grad_out, route_weight, routes, w_gate, w_up, w_down):
    n_ctx, n_exp, n_etp = (lax.axis_size(name) for name in ("ctx", "exp", "etp"))
    rows, feats = tokens.shape
    hid, full = w_gate.shape
    slots = n_exp * MOST
    n_x = n_etp // 2
    chunks = n_exp // 2
    acts_rows = -(-3 * hid // (16 * LANES)) * 16 * LANES
    lane_rows = acts_rows // LANES
    vmem = pl.BlockSpec(memory_space=pltpu.VMEM)
    hbm = pl.BlockSpec(memory_space=pl.ANY)
    dma = pltpu.SemaphoreType.DMA
    steps = n_ctx - 1
    grad_shape = jax.ShapeDtypeStruct((hid, feats), BF16)
    return pl.pallas_call(
        functools.partial(kernel, n_ctx, n_exp, n_etp),
        out_shape=(jax.ShapeDtypeStruct((rows, feats), BF16), grad_shape, grad_shape, grad_shape),
        in_specs=[vmem] * 4 + [hbm] * 3,
        out_specs=(vmem,) * 4,
        scratch_shapes=[
            pltpu.VMEM((n_exp * rows, 2 * feats + TAG), BF16),
            pltpu.VMEM((2, slots, full), BF16),
            pltpu.VMEM((hid, full), BF16),
            pltpu.VMEM((hid, full), BF16),
            pltpu.VMEM((hid, full), BF16),
            pltpu.VMEM((acts_rows, slots), BF16),
            pltpu.VMEM((acts_rows, feats), F32),
            pltpu.VMEM((LANES, steps, lane_rows, feats), BF16),
            pltpu.VMEM((LANES, steps, lane_rows, feats), BF16),
            pltpu.VMEM((n_x, slots, feats), BF16),
            pltpu.VMEM((n_x, slots, feats), BF16),
            pltpu.VMEM((slots, feats), BF16),
            pltpu.VMEM((2, slots // 2, feats), BF16),
            pltpu.VMEM((3, slots, feats), F32),
            pltpu.VMEM((2, slots, feats), BF16),
            pltpu.VMEM((2, slots, feats), BF16),
            pltpu.VMEM((slots, feats), BF16),
            pltpu.VMEM((n_exp, MOST, feats), BF16),
            dma((3,)),
            dma((n_exp, 2)),
            dma((n_exp, 2)),
            dma((9, chunks)),
            dma((9, chunks)),
            dma((LANES, steps)),
            dma((LANES, steps)),
            dma((n_x,)),
            dma((n_x,)),
            dma((2,)),
            dma((2,)),
            dma((2,)),
            dma((2,)),
            dma((n_exp,)),
            dma((n_exp,)),
        ],
        compiler_params=pltpu.CompilerParams(
            collective_id=0, has_side_effects=True, vmem_limit_bytes=48 * 1024 * 1024
        ),
        name="expert_backward",
    )(tokens, grad_out, route_weight, routes, w_gate, w_up, w_down)


def solution(mesh):
    in_specs = (
        P(("ctx", "exp"), "etp"),
        P(("ctx", "exp"), "etp"),
        P(("ctx", "exp"), None),
        P(("ctx", "exp"), None),
        P(("exp", "etp"), None),
        P(("exp", "etp"), None),
        P(("exp", "etp"), None),
    )
    out_specs = (
        P(("ctx", "exp"), "etp"),
        P(("exp", "etp"), "ctx"),
        P(("exp", "etp"), "ctx"),
        P(("exp", "etp"), "ctx"),
    )
    return jax.shard_map(
        on_device, mesh=mesh, in_specs=in_specs, out_specs=out_specs, check_vma=False
    )
```

```python
import functools

import jax
import jax.numpy as jnp
from jax import lax
from jax.experimental import pallas as pl
from jax.experimental.pallas import tpu as pltpu
from jax.sharding import PartitionSpec as P

EXPERTS = 4
MOST = 16
TAG = 128
LANES = 4
LAG_NEAR = 2
LAG_FAR = 3
LAG_SWAP = 3
MESH = pl.DeviceIdType.MESH
F32 = jnp.float32
BF16 = jnp.bfloat16
ACROSS = (((1,), (1,)), ((), ()))
LEADING = (((0,), (0,)), ((), ()))


def aligned(index, size):
    return pl.ds(pl.multiple_of(index * size, size), size)


def kernel(
    n_ctx,
    n_exp,
    n_etp,
    tok_hbm,
    grad_hbm,
    weight_hbm,
    routes_hbm,
    gate_hbm,
    up_hbm,
    down_hbm,
    d_tok_ref,
    d_gate_ref,
    d_up_ref,
    d_down_ref,
    grad_vmem,
    weight_vmem,
    routes_vmem,
    raw,
    raw_swap,
    x,
    x_swap,
    w_gate,
    w_up,
    w_down,
    acts,
    pair_out,
    pair_in,
    far_out,
    far_in,
    near_sum,
    near_out,
    near_in,
    home_out,
    home_in,
    w_sem,
    swap_send,
    swap_recv,
    z_send,
    z_recv,
    zs_send,
    zs_recv,
    x_send,
    x_recv,
    xs_send,
    xs_recv,
    y_send,
    y_recv,
    pair_send,
    pair_recv,
    far_send,
    far_recv,
    near_send,
    near_recv,
    home_send,
    home_recv,
):
    rows, feats = grad_vmem.shape
    hid = w_gate.shape[0]
    half = rows // 2
    n_x = n_etp // 2
    group_split = n_exp // EXPERTS
    chunks = n_exp // 2
    slots = n_exp * MOST
    c = lax.axis_index("ctx")
    z = lax.axis_index("exp")
    t = lax.axis_index("etp")
    xx = t // 2
    core = t % 2
    sib = t + 1 - 2 * core
    expert = z // group_split

    def along_x(step):
        return ((xx + step) % n_x) * 2 + core

    right, left, far = along_x(1), along_x(n_x - 1), along_x(2)
    z_next, z_prev = (z + 1) % n_exp, (z + n_exp - 1) % n_exp
    y_next, y_prev = (c + 1) % n_ctx, (c + n_ctx - 1) % n_ctx

    barrier = pltpu.get_barrier_semaphore()
    partners = [
        {"etp": right},
        {"etp": left},
        {"etp": sib},
        {"ctx": y_next},
        {"ctx": y_prev},
        {"exp": z_next},
        {"exp": z_prev},
    ]
    for partner in partners:
        pl.semaphore_signal(barrier, inc=1, device_id=partner, device_id_type=MESH)

    mirror = {"ctx": t, "etp": c}

    @pl.when(c != t)
    def _():
        pl.semaphore_signal(barrier, inc=1, device_id=mirror, device_id_type=MESH)

    small = [
        (tok_hbm, raw.at[pl.ds(0, rows), pl.ds(0, feats)]),
        (grad_hbm, grad_vmem),
        (weight_hbm, weight_vmem),
        (routes_hbm, routes_vmem),
    ]
    loads = [
        pltpu.make_async_copy(src, dst, w_sem.at[i])
        for i, (src, dst) in enumerate(
            small + [(gate_hbm, w_gate), (up_hbm, w_up), (down_hbm, w_down)]
        )
    ]
    for load in loads:
        load.start()
    for load in loads[: len(small)]:
        load.wait()

    square = (rows, rows)
    to_row = lax.broadcasted_iota(jnp.int32, square, 0)
    to_col = lax.broadcasted_iota(jnp.int32, square, 1)

    def as_column(row):
        return jnp.sum(jnp.where(to_row == to_col, row, jnp.zeros_like(row)), axis=1, keepdims=True)

    expert_col = as_column(routes_vmem[...].astype(F32))
    scale = as_column(weight_vmem[...])
    lane = lax.broadcasted_iota(jnp.int32, (rows, TAG), 1).astype(F32)
    one_hot = jnp.where(lane == expert_col, 1.0, 0.0)
    earlier = jnp.where(to_row > to_col, 1.0, 0.0).astype(BF16)
    before = jnp.dot(earlier, one_hot.astype(BF16), preferred_element_type=F32)
    rank = jnp.sum(before * one_hot, axis=1, keepdims=True)
    position = expert_col * MOST + rank
    raw[:rows, feats : 2 * feats] = (scale * grad_vmem[...].astype(F32)).astype(BF16)
    raw[:rows, 2 * feats :] = jnp.broadcast_to(position, (rows, TAG)).astype(BF16)

    @pl.when(c != t)
    def _():
        pl.semaphore_wait(barrier, len(partners) + 1)

    @pl.when(c == t)
    def _():
        pl.semaphore_wait(barrier, len(partners))

    def send(src, dst, send_sem, recv_sem, target):
        return pltpu.make_async_remote_copy(
            src_ref=src,
            dst_ref=dst,
            send_sem=send_sem,
            recv_sem=recv_sem,
            device_id=target,
            device_id_type=MESH,
        )

    def swap_copy():
        return send(
            raw.at[pl.ds(0, rows)], raw_swap.at[pl.ds(0, rows)], swap_send, swap_recv, mirror
        )

    def raw_half(block, part):
        return raw.at[aligned(2 * block + part, half)]

    def z_copy(src, dst, part, target):
        return send(
            raw_half(src, part),
            raw_half(dst, part),
            z_send.at[dst, part],
            z_recv.at[dst, part],
            {"exp": target},
        )

    for part in range(2):
        z_copy(0, 1, part, z_next).start()
        z_copy(0, 2, part, z_prev).start()

    @pl.when(c != t)
    def _():
        swap_copy().start()

    @pl.when(c == t)
    def _():
        raw_swap[:rows, :] = raw[:rows, :]

    def zs_copy(src, dst, target):
        return send(
            raw_swap.at[aligned(src, rows)],
            raw_swap.at[aligned(dst, rows)],
            zs_send.at[dst],
            zs_recv.at[dst],
            {"exp": target},
        )

    chunk_rows = 2 * MOST
    swap_rows = 4 * MOST
    swap_chunks = chunks // 2

    def piece(k, owner):
        return x.at[:, aligned(k, chunk_rows), aligned(owner, feats)]

    def piece_of(kind, k, owner):
        return x.at[kind, aligned(k, chunk_rows), aligned(owner, feats)]

    def swap_piece(k, owner):
        return x_swap.at[:, aligned(owner * swap_chunks + k, swap_rows), :]

    def swap_piece_of(kind, k, owner):
        return x_swap.at[kind, aligned(owner * swap_chunks + k, swap_rows), :]

    def gather(whole, part, send_sem, recv_sem):
        turn = 1 - 2 * core

        def copy(which, k):
            ref, target = (
                lambda: (whole(k, t), right),
                lambda: (whole(k, t), left),
                lambda: (whole(k, t), sib),
                lambda: (part(0, k, left), right),
                lambda: (part(1, k, right), left),
                lambda: (whole(k, left), sib),
                lambda: (whole(k, right), sib),
                lambda: (part(0, k, far), sib),
                lambda: (part(1, k, far), sib),
            )[which]()
            return send(ref, ref, send_sem.at[which, k], recv_sem.at[which, k], {"etp": target})

        def arrive(which, k):
            ref = (
                lambda: whole(k, left),
                lambda: whole(k, right),
                lambda: whole(k, sib),
                lambda: part(0, k, far),
                lambda: part(1, k, far),
                lambda: whole(k, left + turn),
                lambda: whole(k, right + turn),
                lambda: part(0, k, far + turn),
                lambda: part(1, k, far + turn),
            )[which]()
            send(ref, ref, send_sem.at[which, k], recv_sem.at[which, k], {"etp": sib}).wait_recv()

        return copy, arrive

    x_copy, x_arrive = gather(piece, piece_of, x_send, x_recv)
    xs_copy, xs_arrive = gather(swap_piece, swap_piece_of, xs_send, xs_recv)

    def pass_near(copy, arrive, k):
        arrive(0, k)
        copy(3, k).start()
        copy(5, k).start()
        arrive(1, k)
        copy(4, k).start()
        copy(6, k).start()

    def pass_far(copy, arrive, k):
        arrive(3, k)
        copy(7, k).start()
        arrive(4, k)
        copy(8, k).start()

    def finish(copy, arrive, k):
        for which in (2, 5, 6, 7, 8):
            arrive(which, k)
        for which in range(9):
            copy(which, k).wait_send()

    pick_row = lax.broadcasted_iota(jnp.int32, (2 * rows, 2 * MOST), 0)
    pick_lane = lax.broadcasted_iota(jnp.int32, (2 * rows, 2 * MOST), 1)

    def choose(blocks, k):
        block = blocks[aligned(k, 2 * rows), :]
        tag = block[:, 2 * feats : 2 * feats + 2 * MOST].astype(jnp.int32) - expert * MOST
        spot = jnp.where(pick_row >= rows, tag + MOST, tag)
        pick = jnp.where((tag >= 0) & (tag < MOST) & (spot == pick_lane), 1.0, 0.0).astype(BF16)
        return lax.dot_general(
            pick, block[:, : 2 * feats], LEADING, preferred_element_type=F32
        ).astype(BF16)

    def dispatch(i, carry):
        @pl.when(i < chunks)
        def _():
            forth, back = 2 * i + 1, 2 * i + 2
            for part in range(2):
                z_copy(forth, forth, part, z_next).wait_recv()

                @pl.when(i < chunks - 1)
                def _():
                    z_copy(forth, forth + 2, part, z_next).start()
                    z_copy(back, back, part, z_prev).wait_recv()

                @pl.when(i < chunks - 2)
                def _():
                    z_copy(back, back + 2, part, z_prev).start()

            chosen = choose(raw, i)
            x[0, aligned(i, chunk_rows), aligned(t, feats)] = chosen[:, :feats]
            x[1, aligned(i, chunk_rows), aligned(t, feats)] = chosen[:, feats:]
            for which in range(3):
                x_copy(which, i).start()

        @pl.when((i >= LAG_NEAR) & (i < chunks + LAG_NEAR))
        def _():
            pass_near(x_copy, x_arrive, i - LAG_NEAR)

        @pl.when(i >= LAG_FAR)
        def _():
            pass_far(x_copy, x_arrive, i - LAG_FAR)

        @pl.when(i == LAG_SWAP - 1)
        def _():
            @pl.when(c != t)
            def _():
                swap_copy().wait_recv()

            zs_copy(0, 1, z_next).start()
            zs_copy(0, 2, z_prev).start()

        @pl.when(i >= LAG_SWAP)
        def _():
            k = i - LAG_SWAP
            forth, back = 2 * k + 1, 2 * k + 2
            zs_copy(forth, forth, z_next).wait_recv()

            @pl.when(k < chunks - 1)
            def _():
                zs_copy(forth, forth + 2, z_next).start()
                zs_copy(back, back, z_prev).wait_recv()

            @pl.when(k < chunks - 2)
            def _():
                zs_copy(back, back + 2, z_prev).start()

            chosen = choose(raw_swap, k)
            x_swap[0, aligned(t * chunks + k, chunk_rows), :] = chosen[:, :feats]
            x_swap[1, aligned(t * chunks + k, chunk_rows), :] = chosen[:, feats:]

            @pl.when(k % 2 == 1)
            def _():
                for which in range(3):
                    xs_copy(which, k // 2).start()

        return carry

    lax.fori_loop(0, chunks + LAG_FAR, dispatch, 0)

    def gathered(k, carry):
        finish(x_copy, x_arrive, k)
        return carry

    lax.fori_loop(0, chunks, gathered, 0)
    for load in loads[len(small) :]:
        load.wait()

    tok_all, grad_all = x[0], x[1]
    gate = lax.dot_general(w_gate[...], tok_all, ACROSS, preferred_element_type=F32)
    up = lax.dot_general(w_up[...], tok_all, ACROSS, preferred_element_type=F32)
    d_hidden = lax.dot_general(w_down[...], grad_all, ACROSS, preferred_element_type=F32)
    sig = jax.nn.sigmoid(gate)
    activated = gate * sig
    hidden = activated * up
    d_gate = d_hidden * up * sig * (1.0 + gate * (1.0 - sig))
    d_up = d_hidden * activated
    acts_rows = acts.shape[0]
    acts[:, aligned(c, slots)] = jnp.concatenate(
        [d_gate, d_up, hidden, jnp.zeros((acts_rows - 3 * hid, slots), F32)], axis=0
    ).astype(BF16)
    wide = -(-hid // 128) * 128
    fill = jnp.zeros((wide - hid, slots), F32)
    gate_act = jnp.concatenate([d_gate, fill], axis=0).T.astype(BF16)[:, :hid]
    up_act = jnp.concatenate([d_up, fill], axis=0).T.astype(BF16)[:, :hid]

    lane_rows = acts_rows // LANES

    full_hops = (n_ctx - 1) // 2

    def y_copy(side, hop, lane_of):
        owner = (c + hop) % n_ctx if side else (c + n_ctx - hop) % n_ctx
        ref = acts.at[pl.ds(lane_of * lane_rows, lane_rows), aligned(owner, slots)]
        return send(
            ref,
            ref,
            y_send.at[side, hop, lane_of],
            y_recv.at[side, hop, lane_of],
            {"ctx": y_prev if side else y_next},
        )

    def y_arrive(side, hop, lane_of):
        owner = (c + hop + 1) % n_ctx if side else (c + n_ctx - hop - 1) % n_ctx
        ref = acts.at[pl.ds(lane_of * lane_rows, lane_rows), aligned(owner, slots)]
        send(
            ref,
            ref,
            y_send.at[side, hop, lane_of],
            y_recv.at[side, hop, lane_of],
            {"ctx": y_prev if side else y_next},
        ).wait_recv()

    def y_order(hop):
        if hop < full_hops:
            return [(side, lane_of) for lane_of in range(LANES) for side in range(2)]
        return [(side, 2 * lane_of + side) for lane_of in range(LANES // 2) for side in range(2)]

    def y_hop(hop):
        sends = y_order(hop) if hop <= full_hops else []
        waits = y_order(hop - 1) if hop > 0 else []
        for which in waits or sends:
            if which in waits:
                y_arrive(which[0], hop - 1, which[1])
            if which in sends:
                y_copy(which[0], hop, which[1]).start()

    def slot_part(owner):
        cols = aligned(owner, feats)
        return jnp.dot(gate_act, w_gate[:, cols], preferred_element_type=F32) + jnp.dot(
            up_act, w_up[:, cols], preferred_element_type=F32
        )

    def pair_copy(i):
        return send(
            pair_out.at[i], pair_in.at[i], pair_send.at[i], pair_recv.at[i], {"etp": sib}
        )

    middle = slots // 2

    def far_copy(side):
        return send(
            far_out.at[pl.ds(side * middle, middle)],
            far_in.at[side],
            far_send.at[side],
            far_recv.at[side],
            {"etp": left if side else right},
        )

    def near_copy(side):
        return send(
            near_out.at[side],
            near_in.at[side],
            near_send.at[side],
            near_recv.at[side],
            {"etp": left if side else right},
        )

    def to_pair():
        for i in (2, 1, 3, 0):
            pair_out[i] = slot_part(((xx + i) % n_x) * 2 + 1 - core).astype(BF16)
            pair_copy(i).start()

    def pair_sum(i):
        value = slot_part(along_x(i))
        pair_copy(i).wait_recv()
        return value + pair_in[i].astype(F32)

    def to_far():
        far_out[...] = pair_sum(2).astype(BF16)
        far_copy(0).start()
        far_copy(1).start()
        near_sum[0] = pair_sum(1)
        near_sum[1] = pair_sum(n_x - 1)

    def to_near():
        far_copy(0).wait_recv()
        near_out[0, :middle, :] = (near_sum[0, :middle, :] + far_in[0].astype(F32)).astype(BF16)
        near_out[0, middle:, :] = near_sum[0, middle:, :].astype(BF16)
        near_copy(0).start()
        far_copy(1).wait_recv()
        near_out[1, :middle, :] = near_sum[1, :middle, :].astype(BF16)
        near_out[1, middle:, :] = (near_sum[1, middle:, :] + far_in[1].astype(F32)).astype(BF16)
        near_copy(1).start()
        near_sum[2] = pair_sum(0)

    def shift(block):
        k = (block + 1) // 2
        return -k if block % 2 else k

    def home_copy(block):
        return send(
            home_out.at[pl.ds(block * MOST, MOST)],
            home_in.at[z],
            home_send.at[block],
            home_recv.at[block],
            {"exp": (z + shift(block) + n_exp) % n_exp},
        )

    def to_home():
        near_copy(0).wait_recv()
        near_copy(1).wait_recv()
        home_out[...] = (
            near_sum[2] + near_in[0].astype(F32) + near_in[1].astype(F32)
        ).astype(BF16)
        for block in range(1, n_exp):
            home_copy(block).start()
        home_in[z] = home_out[:MOST, :]

    def at_home():
        for block in range(1, n_exp):
            source = (z - shift(block) + n_exp) % n_exp
            ref = home_in.at[source]
            send(ref, ref, home_send.at[block], home_recv.at[block], {"exp": source}).wait_recv()
        merged = []
        for e in range(EXPERTS):
            value = home_in[e * group_split].astype(F32)
            for j in range(1, group_split):
                value = value + home_in[e * group_split + j].astype(F32)
            merged.append(value)
        merged = jnp.concatenate(merged, axis=0).astype(BF16)
        spots = EXPERTS * MOST
        place = jnp.where(
            lax.broadcasted_iota(jnp.int32, (rows, spots), 1) == position.astype(jnp.int32), 1.0, 0.0
        ).astype(BF16)
        d_tok_ref[...] = jnp.dot(place, merged, preferred_element_type=F32).astype(BF16)

    def swap_near(k, carry):
        pass_near(xs_copy, xs_arrive, k)
        return carry

    def swap_far(k, carry):
        pass_far(xs_copy, xs_arrive, k)
        return carry

    def swap_finish(k, carry):
        finish(xs_copy, xs_arrive, k)
        return carry

    y_hop(0)
    to_pair()
    to_far()
    y_hop(1)
    to_near()
    lax.fori_loop(0, swap_chunks, swap_near, 0)
    y_hop(2)
    to_home()
    lax.fori_loop(0, swap_chunks, swap_far, 0)
    y_hop(3)
    lax.fori_loop(0, swap_chunks, swap_finish, 0)
    y_hop(4)
    d_gate_ref[...] = jnp.dot(acts[:hid, :], x_swap[0], preferred_element_type=F32).astype(BF16)
    d_up_ref[...] = jnp.dot(
        acts[hid : 2 * hid, :], x_swap[0], preferred_element_type=F32
    ).astype(BF16)
    d_down_ref[...] = jnp.dot(
        acts[2 * hid : 3 * hid, :], x_swap[1], preferred_element_type=F32
    ).astype(BF16)
    at_home()

    @pl.when(c != t)
    def _():
        swap_copy().wait_send()

    for block in range(1, n_exp):
        for part in range(2):
            z_copy(block, block, part, z_next).wait_send()
        zs_copy(block, block, z_next).wait_send()
        home_copy(block).wait_send()
    for hop in range(full_hops + 1):
        for side, lane_of in y_order(hop):
            y_copy(side, hop, lane_of).wait_send()
    for i in range(n_x):
        pair_copy(i).wait_send()
    for side in range(2):
        far_copy(side).wait_send()
        near_copy(side).wait_send()


def hand_over(*refs):
    count = len(refs) // 2
    for i in range(count):
        refs[count + i][...] = refs[i][...]


def on_device(tokens, grad_out, route_weight, routes, w_gate, w_up, w_down):
    n_ctx, n_exp, n_etp = (lax.axis_size(name) for name in ("ctx", "exp", "etp"))
    rows, feats = tokens.shape
    hid, full = w_gate.shape
    slots = n_exp * MOST
    n_x = n_etp // 2
    chunks = n_exp // 2
    acts_rows = -(-3 * hid // (16 * LANES)) * 16 * LANES
    vmem = pl.BlockSpec(memory_space=pltpu.VMEM)
    hbm = pl.BlockSpec(memory_space=pl.ANY)
    dma = pltpu.SemaphoreType.DMA
    hops = n_ctx // 2
    grad_shape = jax.ShapeDtypeStruct((hid, feats), BF16)
    out_shape = (jax.ShapeDtypeStruct((rows, feats), BF16), grad_shape, grad_shape, grad_shape)
    results = pl.pallas_call(
        functools.partial(kernel, n_ctx, n_exp, n_etp),
        out_shape=out_shape,
        in_specs=[hbm] * 7,
        out_specs=(vmem,) * 4,
        scratch_shapes=[
            pltpu.VMEM((rows, feats), BF16),
            pltpu.VMEM((1, rows), F32),
            pltpu.VMEM((1, rows), jnp.int32),
            pltpu.VMEM((n_exp * rows, 2 * feats + TAG), BF16),
            pltpu.VMEM((n_exp * rows, 2 * feats + TAG), BF16),
            pltpu.VMEM((2, slots, full), BF16),
            pltpu.VMEM((2, n_ctx * slots, feats), BF16),
            pltpu.VMEM((hid, full), BF16),
            pltpu.VMEM((hid, full), BF16),
            pltpu.VMEM((hid, full), BF16),
            pltpu.VMEM((acts_rows, n_ctx * slots), BF16),
            pltpu.VMEM((n_x, slots, feats), BF16),
            pltpu.VMEM((n_x, slots, feats), BF16),
            pltpu.VMEM((slots, feats), BF16),
            pltpu.VMEM((2, slots // 2, feats), BF16),
            pltpu.VMEM((3, slots, feats), F32),
            pltpu.VMEM((2, slots, feats), BF16),
            pltpu.VMEM((2, slots, feats), BF16),
            pltpu.VMEM((slots, feats), BF16),
            pltpu.VMEM((n_exp, MOST, feats), BF16),
            dma((7,)),
            dma,
            dma,
            dma((n_exp, 2)),
            dma((n_exp, 2)),
            dma((n_exp,)),
            dma((n_exp,)),
            dma((9, chunks)),
            dma((9, chunks)),
            dma((9, chunks // 2)),
            dma((9, chunks // 2)),
            dma((2, hops, LANES)),
            dma((2, hops, LANES)),
            dma((n_x,)),
            dma((n_x,)),
            dma((2,)),
            dma((2,)),
            dma((2,)),
            dma((2,)),
            dma((n_exp,)),
            dma((n_exp,)),
        ],
        compiler_params=pltpu.CompilerParams(
            collective_id=0, has_side_effects=True, vmem_limit_bytes=60 * 1024 * 1024
        ),
        name="expert_backward",
    )(tokens, grad_out, route_weight.reshape(1, rows), routes.reshape(1, rows), w_gate, w_up, w_down)
    return pl.pallas_call(
        hand_over,
        out_shape=out_shape,
        in_specs=[vmem] * 4,
        out_specs=(vmem,) * 4,
        name="hand_over",
    )(*results)


def solution(mesh):
    in_specs = (
        P(("ctx", "exp"), "etp"),
        P(("ctx", "exp"), "etp"),
        P(("ctx", "exp"), None),
        P(("ctx", "exp"), None),
        P(("exp", "etp"), None),
        P(("exp", "etp"), None),
        P(("exp", "etp"), None),
    )
    out_specs = (
        P(("ctx", "exp"), "etp"),
        P(("exp", "etp"), "ctx"),
        P(("exp", "etp"), "ctx"),
        P(("exp", "etp"), "ctx"),
    )
    return jax.shard_map(
        on_device, mesh=mesh, in_specs=in_specs, out_specs=out_specs, check_vma=False
    )
```

```python
import functools

import jax
import jax.numpy as jnp
from jax import lax
from jax.experimental import pallas as pl
from jax.experimental.pallas import tpu as pltpu
from jax.sharding import PartitionSpec as P

EXPERTS = 4
MOST = 16
TAG = 128
LANES = 2
PARTS = 2
LAG_NEAR = 1
LAG_FAR = 3
LAG_SWAP = 3
MESH = pl.DeviceIdType.MESH
F32 = jnp.float32
BF16 = jnp.bfloat16
ACROSS = (((1,), (1,)), ((), ()))
LEADING = (((0,), (0,)), ((), ()))


def when(condition):
    if isinstance(condition, bool):
        return lambda body: body() if condition else None
    return pl.when(condition)


def aligned(index, size):
    return pl.ds(pl.multiple_of(index * size, size), size)


def kernel(
    n_ctx,
    n_exp,
    n_etp,
    tok_hbm,
    grad_hbm,
    weight_hbm,
    routes_hbm,
    gate_hbm,
    up_hbm,
    down_hbm,
    d_tok_ref,
    d_gate_ref,
    d_up_ref,
    d_down_ref,
    grad_vmem,
    weight_vmem,
    routes_vmem,
    raw,
    raw_swap,
    x,
    x_swap,
    w_gate,
    w_up,
    w_down,
    acts,
    pair_out,
    pair_in,
    far_out,
    far_in,
    near_sum,
    near_out,
    near_in,
    home_out,
    home_in,
    w_sem,
    swap_send,
    swap_recv,
    z_send,
    z_recv,
    zs_send,
    zs_recv,
    x_send,
    x_recv,
    xs_send,
    xs_recv,
    y_send,
    y_recv,
    pair_send,
    pair_recv,
    far_send,
    far_recv,
    near_send,
    near_recv,
    home_send,
    home_recv,
):
    rows, feats = grad_vmem.shape
    hid = w_gate.shape[0]
    half = rows // 2
    n_x = n_etp // 2
    group_split = n_exp // EXPERTS
    chunks = n_exp // 2
    slots = n_exp * MOST
    c = lax.axis_index("ctx")
    z = lax.axis_index("exp")
    t = lax.axis_index("etp")
    xx = t // 2
    core = t % 2
    sib = t + 1 - 2 * core
    expert = z // group_split

    def along_x(step):
        return ((xx + step) % n_x) * 2 + core

    right, left, far = along_x(1), along_x(n_x - 1), along_x(2)
    z_next, z_prev = (z + 1) % n_exp, (z + n_exp - 1) % n_exp
    y_next, y_prev = (c + 1) % n_ctx, (c + n_ctx - 1) % n_ctx

    barrier = pltpu.get_barrier_semaphore()
    partners = [
        {"etp": right},
        {"etp": left},
        {"etp": sib},
        {"ctx": y_next},
        {"ctx": y_prev},
        {"exp": z_next},
        {"exp": z_prev},
    ]
    for partner in partners:
        pl.semaphore_signal(barrier, inc=1, device_id=partner, device_id_type=MESH)

    mirror = {"ctx": t, "etp": c}

    @pl.when(c != t)
    def _():
        pl.semaphore_signal(barrier, inc=1, device_id=mirror, device_id_type=MESH)

    small = [
        (tok_hbm, raw.at[pl.ds(0, rows), pl.ds(0, feats)]),
        (grad_hbm, grad_vmem),
        (weight_hbm, weight_vmem),
        (routes_hbm, routes_vmem),
    ]
    loads = [
        pltpu.make_async_copy(src, dst, w_sem.at[i])
        for i, (src, dst) in enumerate(
            small + [(gate_hbm, w_gate), (up_hbm, w_up), (down_hbm, w_down)]
        )
    ]
    for load in loads:
        load.start()
    for load in loads[: len(small)]:
        load.wait()

    square = (rows, rows)
    to_row = lax.broadcasted_iota(jnp.int32, square, 0)
    to_col = lax.broadcasted_iota(jnp.int32, square, 1)

    def as_column(row):
        return jnp.sum(jnp.where(to_row == to_col, row, jnp.zeros_like(row)), axis=1, keepdims=True)

    expert_col = as_column(routes_vmem[...].astype(F32))
    scale = as_column(weight_vmem[...])
    lane = lax.broadcasted_iota(jnp.int32, (rows, TAG), 1).astype(F32)
    one_hot = jnp.where(lane == expert_col, 1.0, 0.0)
    earlier = jnp.where(to_row > to_col, 1.0, 0.0).astype(BF16)
    before = jnp.dot(earlier, one_hot.astype(BF16), preferred_element_type=F32)
    rank = jnp.sum(before * one_hot, axis=1, keepdims=True)
    position = expert_col * MOST + rank
    raw[:rows, feats : 2 * feats] = (scale * grad_vmem[...].astype(F32)).astype(BF16)
    raw[:rows, 2 * feats :] = jnp.broadcast_to(position, (rows, TAG)).astype(BF16)

    @pl.when(c != t)
    def _():
        pl.semaphore_wait(barrier, len(partners) + 1)

    @pl.when(c == t)
    def _():
        pl.semaphore_wait(barrier, len(partners))

    def send(src, dst, send_sem, recv_sem, target):
        return pltpu.make_async_remote_copy(
            src_ref=src,
            dst_ref=dst,
            send_sem=send_sem,
            recv_sem=recv_sem,
            device_id=target,
            device_id_type=MESH,
        )

    def swap_copy():
        return send(
            raw.at[pl.ds(0, rows)], raw_swap.at[pl.ds(0, rows)], swap_send, swap_recv, mirror
        )

    def raw_half(block, part):
        return raw.at[aligned(2 * block + part, half)]

    def z_copy(src, dst, part, target):
        return send(
            raw_half(src, part),
            raw_half(dst, part),
            z_send.at[dst, part],
            z_recv.at[dst, part],
            {"exp": target},
        )

    for part in range(2):
        z_copy(0, 1, part, z_next).start()
        z_copy(0, 2, part, z_prev).start()

    @pl.when(c != t)
    def _():
        swap_copy().start()

    @pl.when(c == t)
    def _():
        raw_swap[:rows, :] = raw[:rows, :]

    def zs_copy(src, dst, target):
        return send(
            raw_swap.at[aligned(src, rows)],
            raw_swap.at[aligned(dst, rows)],
            zs_send.at[dst],
            zs_recv.at[dst],
            {"exp": target},
        )

    chunk_rows = 2 * MOST
    swap_rows = 4 * MOST
    swap_chunks = chunks // 2

    def piece(k, owner):
        return x.at[:, aligned(k, chunk_rows), aligned(owner, feats)]

    def piece_of(kind, k, owner):
        return x.at[kind, aligned(k, chunk_rows), aligned(owner, feats)]

    def swap_piece(k, owner):
        return x_swap.at[:, aligned(owner * swap_chunks + k, swap_rows), :]

    def swap_piece_of(kind, k, owner):
        return x_swap.at[kind, aligned(owner * swap_chunks + k, swap_rows), :]

    def gather(whole, part, send_sem, recv_sem):
        turn = 1 - 2 * core

        def copy(which, k):
            ref, target = (
                lambda: (whole(k, t), right),
                lambda: (whole(k, t), left),
                lambda: (whole(k, t), sib),
                lambda: (part(0, k, left), right),
                lambda: (part(1, k, right), left),
                lambda: (whole(k, left), sib),
                lambda: (whole(k, right), sib),
                lambda: (part(0, k, far), sib),
                lambda: (part(1, k, far), sib),
            )[which]()
            return send(ref, ref, send_sem.at[which, k], recv_sem.at[which, k], {"etp": target})

        def arrive(which, k):
            ref = (
                lambda: whole(k, left),
                lambda: whole(k, right),
                lambda: whole(k, sib),
                lambda: part(0, k, far),
                lambda: part(1, k, far),
                lambda: whole(k, left + turn),
                lambda: whole(k, right + turn),
                lambda: part(0, k, far + turn),
                lambda: part(1, k, far + turn),
            )[which]()
            send(ref, ref, send_sem.at[which, k], recv_sem.at[which, k], {"etp": sib}).wait_recv()

        return copy, arrive

    x_copy, x_arrive = gather(piece, piece_of, x_send, x_recv)
    xs_copy, xs_arrive = gather(swap_piece, swap_piece_of, xs_send, xs_recv)

    def pass_near(copy, arrive, k):
        arrive(0, k)
        copy(3, k).start()
        copy(5, k).start()
        arrive(1, k)
        copy(4, k).start()
        copy(6, k).start()

    def pass_far(copy, arrive, k):
        arrive(3, k)
        copy(7, k).start()
        arrive(4, k)
        copy(8, k).start()

    def finish(copy, arrive, k):
        for which in (2, 5, 6, 7, 8):
            arrive(which, k)
        for which in range(9):
            copy(which, k).wait_send()

    pick_row = lax.broadcasted_iota(jnp.int32, (2 * rows, 2 * MOST), 0)
    pick_lane = lax.broadcasted_iota(jnp.int32, (2 * rows, 2 * MOST), 1)

    def choose(blocks, k):
        block = blocks[aligned(k, 2 * rows), :]
        tag = block[:, 2 * feats : 2 * feats + 2 * MOST].astype(jnp.int32) - expert * MOST
        spot = jnp.where(pick_row >= rows, tag + MOST, tag)
        pick = jnp.where((tag >= 0) & (tag < MOST) & (spot == pick_lane), 1.0, 0.0).astype(BF16)
        return lax.dot_general(
            pick, block[:, : 2 * feats], LEADING, preferred_element_type=F32
        ).astype(BF16)

    def swap_step(k):
        forth, back = 2 * k + 1, 2 * k + 2
        zs_copy(forth, forth, z_next).wait_recv()

        @when(k < chunks - 1)
        def _():
            zs_copy(forth, forth + 2, z_next).start()
            zs_copy(back, back, z_prev).wait_recv()

        @when(k < chunks - 2)
        def _():
            zs_copy(back, back + 2, z_prev).start()

        chosen = choose(raw_swap, k)
        x_swap[0, aligned(t * chunks + k, chunk_rows), :] = chosen[:, :feats]
        x_swap[1, aligned(t * chunks + k, chunk_rows), :] = chosen[:, feats:]

        @when(k % 2 == 1)
        def _():
            for which in range(3):
                xs_copy(which, k // 2).start()

    def dispatch(i, carry):
        forth, back = 2 * i + 1, 2 * i + 2
        for part in range(2):
            z_copy(forth, forth, part, z_next).wait_recv()

            @pl.when(i < chunks - 1)
            def _():
                z_copy(forth, forth + 2, part, z_next).start()
                z_copy(back, back, part, z_prev).wait_recv()

            @pl.when(i < chunks - 2)
            def _():
                z_copy(back, back + 2, part, z_prev).start()

        chosen = choose(raw, i)
        x[0, aligned(i, chunk_rows), aligned(t, feats)] = chosen[:, :feats]
        x[1, aligned(i, chunk_rows), aligned(t, feats)] = chosen[:, feats:]
        for which in range(3):
            x_copy(which, i).start()

        @pl.when(i >= LAG_NEAR)
        def _():
            pass_near(x_copy, x_arrive, i - LAG_NEAR)

        @pl.when(i >= LAG_FAR)
        def _():
            pass_far(x_copy, x_arrive, i - LAG_FAR)

        @pl.when(i == LAG_SWAP - 1)
        def _():
            @pl.when(c != t)
            def _():
                swap_copy().wait_recv()

            zs_copy(0, 1, z_next).start()
            zs_copy(0, 2, z_prev).start()

        @pl.when(i >= LAG_SWAP)
        def _():
            swap_step(i - LAG_SWAP)

        return carry

    lax.fori_loop(0, chunks, dispatch, 0)

    def gathered(k, carry):
        finish(x_copy, x_arrive, k)
        return carry


    acts_rows = acts.shape[0]
    part_slots = slots // PARTS
    wide = -(-hid // 128) * 128
    fill = jnp.zeros((wide - hid, part_slots), F32)
    turned = {}

    def forward(part):
        here = pl.ds(part * part_slots, part_slots)
        gate = lax.dot_general(w_gate[...], x[0, here, :], ACROSS, preferred_element_type=F32)
        up = lax.dot_general(w_up[...], x[0, here, :], ACROSS, preferred_element_type=F32)
        d_hidden = lax.dot_general(w_down[...], x[1, here, :], ACROSS, preferred_element_type=F32)
        sig = jax.nn.sigmoid(gate)
        activated = gate * sig
        hidden = activated * up
        d_gate = d_hidden * up * sig * (1.0 + gate * (1.0 - sig))
        d_up = d_hidden * activated
        acts[:, aligned(c * PARTS + part, part_slots)] = jnp.concatenate(
            [d_gate, d_up, hidden, jnp.zeros((acts_rows - 3 * hid, part_slots), F32)], axis=0
        ).astype(BF16)
        turned[part] = tuple(
            jnp.concatenate([value, fill], axis=0).T.astype(BF16)[:, :hid]
            for value in (d_gate, d_up)
        )

    lane_rows = acts_rows // LANES

    full_hops = (n_ctx - 1) // 2

    def y_block(part, owner, lane_of):
        return acts.at[
            pl.ds(lane_of * lane_rows, lane_rows), aligned(owner * PARTS + part, part_slots)
        ]

    def y_send_of(part, side, hop, lane_of, ref):
        return send(
            ref,
            ref,
            y_send.at[part, side, hop, lane_of],
            y_recv.at[part, side, hop, lane_of],
            {"ctx": y_prev if side else y_next},
        )

    def y_copy(part, side, hop, lane_of):
        owner = (c + hop) % n_ctx if side else (c + n_ctx - hop) % n_ctx
        return y_send_of(part, side, hop, lane_of, y_block(part, owner, lane_of))

    def y_arrive(part, side, hop, lane_of):
        owner = (c + hop + 1) % n_ctx if side else (c + n_ctx - hop - 1) % n_ctx
        y_send_of(part, side, hop, lane_of, y_block(part, owner, lane_of)).wait_recv()

    def y_order(hop):
        if hop < full_hops:
            return [(side, lane_of) for lane_of in range(LANES) for side in range(2)]
        return [(side, 2 * lane_of + side) for lane_of in range(LANES // 2) for side in range(2)]

    def y_hop(part, hop):
        sends = y_order(hop) if hop <= full_hops else []
        waits = y_order(hop - 1) if hop > 0 else []
        for which in waits or sends:
            if which in waits:
                y_arrive(part, which[0], hop - 1, which[1])
            if which in sends:
                y_copy(part, which[0], hop, which[1]).start()

    def slot_part(part, owner):
        cols = aligned(owner, feats)
        gate_act, up_act = turned[part]
        return jnp.dot(gate_act, w_gate[:, cols], preferred_element_type=F32) + jnp.dot(
            up_act, w_up[:, cols], preferred_element_type=F32
        )

    def pair_copy(part, i):
        return send(
            pair_out.at[part, i],
            pair_in.at[part, i],
            pair_send.at[part, i],
            pair_recv.at[part, i],
            {"etp": sib},
        )

    middle = part_slots // 2

    def far_copy(part, side):
        return send(
            far_out.at[part, pl.ds(side * middle, middle)],
            far_in.at[part, side],
            far_send.at[part, side],
            far_recv.at[part, side],
            {"etp": left if side else right},
        )

    def near_copy(part, side):
        return send(
            near_out.at[part, side],
            near_in.at[part, side],
            near_send.at[part, side],
            near_recv.at[part, side],
            {"etp": left if side else right},
        )

    def to_pair(part):
        for i in (2, 1, 3, 0):
            owner = ((xx + i) % n_x) * 2 + 1 - core
            pair_out[part, i] = slot_part(part, owner).astype(BF16)
            pair_copy(part, i).start()

    def pair_sum(part, i):
        value = slot_part(part, along_x(i))
        pair_copy(part, i).wait_recv()
        return value + pair_in[part, i].astype(F32)

    def to_far(part):
        far_out[part] = pair_sum(part, 2).astype(BF16)
        far_copy(part, 0).start()
        far_copy(part, 1).start()
        near_sum[part, 0] = pair_sum(part, 1)
        near_sum[part, 1] = pair_sum(part, n_x - 1)

    def to_near(part):
        for side in range(2):
            far_copy(part, side).wait_recv()
            low, high = near_sum[part, side, :middle, :], near_sum[part, side, middle:, :]
            if side:
                high = high + far_in[part, side].astype(F32)
            else:
                low = low + far_in[part, side].astype(F32)
            near_out[part, side, :middle, :] = low.astype(BF16)
            near_out[part, side, middle:, :] = high.astype(BF16)
            near_copy(part, side).start()
        near_sum[part, 2] = pair_sum(part, 0)

    def shift(block):
        k = (block + 1) // 2
        return -k if block % 2 else k

    def home_copy(block):
        return send(
            home_out.at[pl.ds(block * MOST, MOST)],
            home_in.at[z],
            home_send.at[block],
            home_recv.at[block],
            {"exp": (z + shift(block) + n_exp) % n_exp},
        )

    def to_home(part):
        near_copy(part, 0).wait_recv()
        near_copy(part, 1).wait_recv()
        home_out[pl.ds(part * part_slots, part_slots), :] = (
            near_sum[part, 2] + near_in[part, 0].astype(F32) + near_in[part, 1].astype(F32)
        ).astype(BF16)
        per = n_exp // PARTS
        for block in range(per * part, per * (part + 1)):
            if block == 0:
                home_in[z] = home_out[:MOST, :]
            else:
                home_copy(block).start()

    def at_home():
        for block in range(1, n_exp):
            source = (z - shift(block) + n_exp) % n_exp
            ref = home_in.at[source]
            send(ref, ref, home_send.at[block], home_recv.at[block], {"exp": source}).wait_recv()
        merged = []
        for e in range(EXPERTS):
            value = home_in[e * group_split].astype(F32)
            for j in range(1, group_split):
                value = value + home_in[e * group_split + j].astype(F32)
            merged.append(value)
        merged = jnp.concatenate(merged, axis=0).astype(BF16)
        spots = EXPERTS * MOST
        place = jnp.where(
            lax.broadcasted_iota(jnp.int32, (rows, spots), 1) == position.astype(jnp.int32), 1.0, 0.0
        ).astype(BF16)
        d_tok_ref[...] = jnp.dot(place, merged, preferred_element_type=F32).astype(BF16)

    def weights_here():
        for load in loads[len(small) :]:
            load.wait()

    def gather_done(part):
        per = chunks // PARTS
        lax.fori_loop(per * part, per * (part + 1), gathered, 0)

    def swap_done():
        for k in range(swap_chunks):
            finish(xs_copy, xs_arrive, k)

    near = functools.partial(pass_near, x_copy, x_arrive)
    far_on = functools.partial(pass_far, x_copy, x_arrive)
    swap_near = functools.partial(pass_near, xs_copy, xs_arrive)
    swap_far = functools.partial(pass_far, xs_copy, xs_arrive)
    plan = [
        (far_on, 5),
        (weights_here,),
        (gather_done, 0),
        (forward, 0),
        (y_hop, 0, 0),
        (near, 7),
        (to_pair, 0),
        (far_on, 6),
        (swap_step, 5),
        (to_far, 0),
        (far_on, 7),
        (swap_near, 0),
        (swap_step, 6),
        (gather_done, 1),
        (to_near, 0),
        (forward, 1),
        (y_hop, 1, 0),
        (to_pair, 1),
        (swap_step, 7),
        (y_hop, 0, 1),
        (to_home, 0),
        (to_far, 1),
        (swap_near, 1),
        (swap_far, 0),
        (y_hop, 1, 1),
        (to_near, 1),
        (y_hop, 0, 2),
        (swap_near, 2),
        (swap_near, 3),
        (swap_far, 1),
        (to_home, 1),
        (y_hop, 1, 2),
        (y_hop, 0, 3),
        (swap_far, 2),
        (swap_far, 3),
        (y_hop, 1, 3),
        (y_hop, 0, 4),
        (y_hop, 1, 4),
        (swap_done,),
    ]
    for stage in plan:
        stage[0](*stage[1:])
    d_gate_ref[...] = jnp.dot(acts[:hid, :], x_swap[0], preferred_element_type=F32).astype(BF16)
    d_up_ref[...] = jnp.dot(
        acts[hid : 2 * hid, :], x_swap[0], preferred_element_type=F32
    ).astype(BF16)
    d_down_ref[...] = jnp.dot(
        acts[2 * hid : 3 * hid, :], x_swap[1], preferred_element_type=F32
    ).astype(BF16)
    at_home()

    @pl.when(c != t)
    def _():
        swap_copy().wait_send()

    for block in range(1, n_exp):
        for part in range(2):
            z_copy(block, block, part, z_next).wait_send()
        zs_copy(block, block, z_next).wait_send()
        home_copy(block).wait_send()
    for hop in range(full_hops + 1):
        for side, lane_of in y_order(hop):
            for part in range(PARTS):
                y_copy(part, side, hop, lane_of).wait_send()
    for part in range(PARTS):
        for i in range(n_x):
            pair_copy(part, i).wait_send()
        for side in range(2):
            far_copy(part, side).wait_send()
            near_copy(part, side).wait_send()


def hand_over(*refs):
    count = len(refs) // 2
    for i in range(count):
        refs[count + i][...] = refs[i][...]


def on_device(tokens, grad_out, route_weight, routes, w_gate, w_up, w_down):
    n_ctx, n_exp, n_etp = (lax.axis_size(name) for name in ("ctx", "exp", "etp"))
    rows, feats = tokens.shape
    hid, full = w_gate.shape
    slots = n_exp * MOST
    n_x = n_etp // 2
    chunks = n_exp // 2
    acts_rows = -(-3 * hid // (16 * LANES)) * 16 * LANES
    vmem = pl.BlockSpec(memory_space=pltpu.VMEM)
    hbm = pl.BlockSpec(memory_space=pl.ANY)
    dma = pltpu.SemaphoreType.DMA
    hops = n_ctx // 2
    part_slots = slots // PARTS
    grad_shape = jax.ShapeDtypeStruct((hid, feats), BF16)
    out_shape = (jax.ShapeDtypeStruct((rows, feats), BF16), grad_shape, grad_shape, grad_shape)
    results = pl.pallas_call(
        functools.partial(kernel, n_ctx, n_exp, n_etp),
        out_shape=out_shape,
        in_specs=[hbm] * 7,
        out_specs=(vmem,) * 4,
        scratch_shapes=[
            pltpu.VMEM((rows, feats), BF16),
            pltpu.VMEM((1, rows), F32),
            pltpu.VMEM((1, rows), jnp.int32),
            pltpu.VMEM((n_exp * rows, 2 * feats + TAG), BF16),
            pltpu.VMEM((n_exp * rows, 2 * feats + TAG), BF16),
            pltpu.VMEM((2, slots, full), BF16),
            pltpu.VMEM((2, n_ctx * slots, feats), BF16),
            pltpu.VMEM((hid, full), BF16),
            pltpu.VMEM((hid, full), BF16),
            pltpu.VMEM((hid, full), BF16),
            pltpu.VMEM((acts_rows, n_ctx * slots), BF16),
            pltpu.VMEM((PARTS, n_x, part_slots, feats), BF16),
            pltpu.VMEM((PARTS, n_x, part_slots, feats), BF16),
            pltpu.VMEM((PARTS, part_slots, feats), BF16),
            pltpu.VMEM((PARTS, 2, part_slots // 2, feats), BF16),
            pltpu.VMEM((PARTS, 3, part_slots, feats), F32),
            pltpu.VMEM((PARTS, 2, part_slots, feats), BF16),
            pltpu.VMEM((PARTS, 2, part_slots, feats), BF16),
            pltpu.VMEM((slots, feats), BF16),
            pltpu.VMEM((n_exp, MOST, feats), BF16),
            dma((7,)),
            dma,
            dma,
            dma((n_exp, 2)),
            dma((n_exp, 2)),
            dma((n_exp,)),
            dma((n_exp,)),
            dma((9, chunks)),
            dma((9, chunks)),
            dma((9, chunks // 2)),
            dma((9, chunks // 2)),
            dma((PARTS, 2, hops, LANES)),
            dma((PARTS, 2, hops, LANES)),
            dma((PARTS, n_x)),
            dma((PARTS, n_x)),
            dma((PARTS, 2)),
            dma((PARTS, 2)),
            dma((PARTS, 2)),
            dma((PARTS, 2)),
            dma((n_exp,)),
            dma((n_exp,)),
        ],
        compiler_params=pltpu.CompilerParams(
            collective_id=0, has_side_effects=True, vmem_limit_bytes=60 * 1024 * 1024
        ),
        name="expert_backward",
    )(tokens, grad_out, route_weight.reshape(1, rows), routes.reshape(1, rows), w_gate, w_up, w_down)
    return pl.pallas_call(
        hand_over,
        out_shape=out_shape,
        in_specs=[vmem] * 4,
        out_specs=(vmem,) * 4,
        name="hand_over",
    )(*results)


def solution(mesh):
    in_specs = (
        P(("ctx", "exp"), "etp"),
        P(("ctx", "exp"), "etp"),
        P(("ctx", "exp"), None),
        P(("ctx", "exp"), None),
        P(("exp", "etp"), None),
        P(("exp", "etp"), None),
        P(("exp", "etp"), None),
    )
    out_specs = (
        P(("ctx", "exp"), "etp"),
        P(("exp", "etp"), "ctx"),
        P(("exp", "etp"), "ctx"),
        P(("exp", "etp"), "ctx"),
    )
    return jax.shard_map(
        on_device, mesh=mesh, in_specs=in_specs, out_specs=out_specs, check_vma=False
    )
```
